768 devices in a mesh: fsdp: 192 (over y, z_lo, x), tp: 4 (over z_hi, core).
Axes of the slice: x: 4, y: 8, z: 12 (z_hi: 2, z_lo: 6; z = z_hi * 6 + z_lo), core: 2. Of those that a mesh axis runs over, the one named last changes fastest.
Arguments:
- tokens: bfloat16 [49152, 2048], P(('fsdp', 'tp')), may hold values from -6 to 6
- norm_gain: float32 [2048], replicated, may hold values from 0.5 to 1.5
- in_weight: bfloat16 [2048, 6144], P(None, ('fsdp', 'tp')), may hold values from -0.125 to 0.125
- filter_taps: float32 [128, 128], P('tp'), may hold values from -0.5 to 0.5
- skip_gain: float32 [2048], P('tp'), may hold values from 0.5 to 2
Outputs:
- gated: bfloat16 [49152, 2048], P('fsdp', 'tp')
The draws below stay inside these ranges and needn't reach their ends.
All inputs are finite; a program needn't handle non-finite values.
Results may differ from the reference program's by a relative error of at most 0.007.
Values may be sent and summed in bfloat16 or wider, within the bound.
A program may use at most 32 MiB of HBM per device.

```python
import math
import jax
import jax.numpy as jnp
from jax import lax

DIN = 2048
C = 2048
GROUP = 16
TAPS = 128
TOKENS = 49152
GROUPS = 128
N_FSDP = 192
N_TP = 4


def level_of(key, extent, pieces, least, top_value):
    factor_of = 1.0
    for axis_at, shards_of in pieces:
        heights = jax.random.uniform(jax.random.fold_in(jax.random.fold_in(key, 6), axis_at), (shards_of,), jnp.float32, least / len(pieces), top_value / len(pieces))
        factor_of = factor_of * jnp.repeat(jnp.exp(heights), extent[axis_at] // shards_of).reshape((-1,) + (1,) * (len(extent) - 1 - axis_at))
    return factor_of


def normal_values(rng, dims, width, most, cuts=(), kind=jnp.bfloat16):
    values = width * jax.random.normal(rng, dims, jnp.float32)
    if cuts:
        values = values * level_of(rng, dims, cuts, -0.22, 0.18)
    return jnp.clip(values, -most, most).astype(kind)


def setup_inputs(seed: int = 0) -> dict:
    seeds = jax.random.split(jax.random.key(seed), 6)
    return {
        "tokens": normal_values(seeds[0], (TOKENS, DIN), 1.0, 6.0, ((0, 768),)),
        "norm_gain": jnp.clip(1.0 + 0.1 * jax.random.normal(seeds[1], (DIN,), jnp.float32), 0.5, 1.5),
        "in_weight": normal_values(seeds[2], (DIN, 3 * C), DIN ** -0.5, 0.125, ((1, 768),)),
        "filter_taps": normal_values(seeds[3], (GROUPS, TAPS), TAPS ** -0.5, 0.5, ((0, 4),), jnp.float32),
        "skip_gain": jnp.clip(jnp.exp(math.log(2.0) - 1.3862944 * jax.random.uniform(seeds[4], (C,), jnp.float32) ** level_of(seeds[4], (C,), ((0, 4),), -0.2, 0.2)), 0.5, 2.0),
    }


def causal_blocks(extended, filter_taps):
    tap_count = filter_taps.shape[1]
    row_count = extended.shape[0] - tap_count
    channels = extended.shape[1]
    groups = filter_taps.shape[0]
    group_width = channels // groups
    offset = jnp.arange(tap_count)[:, None] - jnp.arange(tap_count)[None, :]
    near_taps = jnp.where(offset >= 0, filter_taps[:, jnp.clip(offset, 0, tap_count - 1)], 0.0)
    far_taps = jnp.where(offset < 0, filter_taps[:, jnp.clip(offset + tap_count, 0, tap_count - 1)], 0.0)
    widened = extended.astype(jnp.float32)
    block_shape = (row_count // tap_count, tap_count, groups, group_width)
    current = widened[tap_count:].reshape(block_shape)
    earlier = widened[:-tap_count].reshape(block_shape)
    result = jnp.einsum('gij,bjgc->bigc', near_taps, current, precision=lax.Precision.HIGHEST)
    result = result + jnp.einsum('gij,bjgc->bigc', far_taps, earlier, precision=lax.Precision.HIGHEST)
    return result.reshape(row_count, channels)

def reference(tokens, norm_gain, in_weight, filter_taps, skip_gain):
    features = tokens.astype(jnp.float32)
    power = lax.optimization_barrier(jnp.mean(features * features, axis=1, keepdims=True))
    normed = (features * lax.rsqrt(power + 1e-06) * norm_gain).astype(jnp.bfloat16)
    per_group = C // N_TP
    block_cols = 3 * C // (N_FSDP * N_TP)
    arranged = in_weight.reshape(DIN, N_FSDP, N_TP, block_cols).transpose(0, 2, 1, 3)
    arranged = arranged.reshape(DIN, N_TP, 3, per_group).transpose(2, 0, 1, 3).reshape(3, DIN, C)
    slice_width = 128
    slices = C // slice_width
    stacked = arranged.reshape(3, DIN, slices, slice_width).transpose(2, 0, 1, 3)
    slice_taps_all = filter_taps.reshape(slices, slice_width // GROUP, TAPS)
    slice_skips_all = skip_gain.reshape(slices, slice_width)

    def one_slice(operands):
        slice_weights, slice_taps, slice_skip = operands
        query = jnp.dot(normed, slice_weights[0], preferred_element_type=jnp.float32)
        keys = jnp.dot(normed, slice_weights[1], preferred_element_type=jnp.float32)
        values = jnp.dot(normed, slice_weights[2], preferred_element_type=jnp.float32)
        mixed = (keys * values).astype(jnp.bfloat16)
        padded = jnp.concatenate([jnp.zeros((TAPS, slice_width), mixed.dtype), mixed], axis=0)
        conv = causal_blocks(padded, slice_taps)
        return (query * (conv + slice_skip * mixed.astype(jnp.float32))).astype(jnp.bfloat16)
    results = lax.map(one_slice, (stacked, slice_taps_all, slice_skips_all))
    return results.transpose(1, 0, 2).reshape(TOKENS, C)
```

```python
import functools

import jax
import jax.numpy as jnp
from jax import lax
from jax.experimental import pallas as pl
from jax.experimental.pallas import tpu as pltpu
from jax.sharding import PartitionSpec as P

MESH = pl.DeviceIdType.MESH
NX, NY, NZ = 4, 8, 6
KC = 4
NT = (((1,), (1,)), ((), ()))


def reach(direction, d):
    return (4 if d < 3 else 3) if direction > 0 else (3 if d < 3 else 4)


def channels():
    names = [("wz", d) for d in range(1, NZ)]
    for d in range(NZ):
        for direction in (1, -1):
            names += [("wy", direction, s, d) for s in range(1, reach(direction, d) + 1)]
    names += [("ox", k) for k in range(1, NX)] + [("os", k) for k in range(NX)]
    for kc in range(KC):
        names += [("cr", kc)]
        names += [("cx", kc, k) for k in range(1, NX)] + [("cs", kc, k) for k in range(NX)]
    names += [("edge",)] + [("out", k) for k in range(1, NX)]
    return {name: i for i, name in enumerate(names)}


CH = channels()


def kernel(
    tokens_ref, gain_ref, w_ref, taps_ref, skip_ref, out_ref,
    tb, wb, acc, toep, skip_b, qb, mx, edge_out, edge_in, send_out, got, ssem, rsem,
):
    f = lax.axis_index("fsdp")
    t = lax.axis_index("tp")
    x = f % NX
    g = f // NX
    zl = g % NZ
    y = g // NZ
    h = t // 2
    c = t % 2
    taps = taps_ref.shape[1]
    chunk = tb.shape[-1]

    def dev(y_, zl_, x_, h_, c_):
        return ((y_ * NZ + zl_) * NX + x_, h_ * 2 + c_)

    def zpeer(d):
        return dev(y, (zl + d) % NZ, x, h, c)

    def ypeer(d):
        return dev((y + d + NY) % NY, zl, x, h, c)

    def xpeer(k):
        return dev(y, zl, (x + k) % NX, h, c)

    sibling = dev(y, zl, x, h, 1 - c)
    partner = dev(y, zl, x, 1 - h, c)
    g_next = (g + 1) % (NY * NZ)
    g_prev = (g + NY * NZ - 1) % (NY * NZ)
    after = dev(g_next // NZ, g_next % NZ, x, h, c)
    before = dev(g_prev // NZ, g_prev % NZ, x, h, c)

    sends = []

    def copy(name, src, dst, to):
        return pltpu.make_async_remote_copy(
            src_ref=src, dst_ref=dst, send_sem=ssem.at[CH[name]], recv_sem=rsem.at[CH[name]],
            device_id=to, device_id_type=MESH,
        )

    def send(name, src, dst, to):
        one = copy(name, src, dst, to)
        one.start()
        sends.append(one)

    def arrived(name, dst):
        copy(name, dst, dst, sibling).wait_recv()

    features = tokens_ref[...].astype(jnp.float32)
    power = jnp.mean(features * features, axis=1, keepdims=True)
    normed = (features * lax.rsqrt(power + 1e-06) * gain_ref[...]).astype(jnp.bfloat16)
    for kc in range(KC):
        tb[kc, 0, x, c] = normed[:, kc * chunk : (kc + 1) * chunk]
    wb[g] = w_ref[...]

    barrier = pltpu.get_barrier_semaphore()
    greet = [zpeer(d) for d in range(1, NZ)] + [ypeer(1), ypeer(-1)]
    greet += [xpeer(k) for k in range(1, NX)] + [sibling, partner, after, before]
    for peer in greet:
        pl.semaphore_signal(barrier, inc=1, device_id=peer, device_id_type=MESH)
    pl.semaphore_wait(barrier, len(greet))

    def column(d):
        return (zl + NZ - d) % NZ

    def block(y_, d):
        return wb.at[y_ * NZ + column(d)]

    def pass_on(direction, s, d):
        if s <= reach(direction, d):
            here = block((y - direction * (s - 1) + NY) % NY, d)
            send(("wy", direction, s, d), here, here, ypeer(direction))

    def on_wz(d):
        arrived(("wz", d), block(y, d))
        pass_on(1, 1, d)
        pass_on(-1, 1, d)

    def on_wy(direction, s, d):
        arrived(("wy", direction, s, d), block((y - direction * s + NY) % NY, d))
        pass_on(direction, s + 1, d)

    def own_piece(k, c_):
        return tb.at[:, 0, (x + NX - k) % NX, c_]

    def far_piece(kc, k, c_):
        return tb.at[kc, 1, (x + NX - k) % NX, c_]

    def on_ox(k):
        piece = own_piece(k, c)
        arrived(("ox", k), piece)
        send(("os", k), piece, piece, sibling)

    def on_cr(kc):
        piece = far_piece(kc, 0, c)
        arrived(("cr", kc), piece)
        for k in (2, 1, 3):
            send(("cx", kc, k), piece, piece, xpeer(k))
        send(("cs", kc, 0), piece, piece, sibling)

    def on_cx(kc, k):
        piece = far_piece(kc, k, c)
        arrived(("cx", kc, k), piece)
        send(("cs", kc, k), piece, piece, sibling)

    here = block(y, 0)
    for d in range(1, NZ):
        send(("wz", d), here, here, zpeer(d))
    pass_on(1, 1, 0)
    pass_on(-1, 1, 0)
    for kc in range(KC):
        send(("cr", kc), tb.at[kc, 0, x, c], tb.at[kc, 1, x, c], partner)
    for k in (2, 1, 3):
        send(("ox", k), own_piece(0, c), own_piece(0, c), xpeer(k))
    send(("os", 0), own_piece(0, c), own_piece(0, c), sibling)

    row_at = lax.broadcasted_iota(jnp.int32, (taps, taps), 0)
    lane_at = lax.broadcasted_iota(jnp.int32, (taps, taps), 1)

    def table(j):
        one = taps_ref[pl.ds(2 * j + x // 2, 1), :]
        rolled = pltpu.roll(jnp.broadcast_to(one, (taps, taps)), 0, 1, stride=1, stride_axis=0)
        toep[j, 0:taps] = jnp.where(lane_at < row_at, rolled, 0.0).astype(jnp.bfloat16)
        toep[j, taps : 2 * taps] = jnp.where(lane_at >= row_at, rolled, 0.0).astype(jnp.bfloat16)

    def skips():
        wide = jnp.broadcast_to(skip_ref[...], (128, skip_ref.shape[1]))
        skip_b[...] = wide.T.reshape(skip_b.shape)

    events = []
    for d in range(1, NZ):
        events.append((1.5 + 1.1 * d, lambda d=d: on_wz(d)))
    for d in range(NZ):
        for direction in (1, -1):
            for s in range(1, reach(direction, d) + 1):
                when = 1.9 * s + 1.1 * d + (1.5 if d else 0.0) + 0.01 * direction
                events.append((when, lambda a=direction, s=s, d=d: on_wy(a, s, d)))
    for k in range(1, NX):
        events.append((11.0 if k == 2 else 8.0, lambda k=k: on_ox(k)))
    for kc in range(KC):
        base = 6.0 + 4.0 * (kc + 1)
        events.append((base, lambda kc=kc: on_cr(kc)))
        for k in range(1, NX):
            events.append((base + (4.0 if k == 2 else 3.5), lambda kc=kc, k=k: on_cx(kc, k)))

    def project(kc, which):
        rows = tb[kc, which].reshape(-1, chunk)
        part = wb[:, :, kc * chunk : (kc + 1) * chunk].reshape(-1, chunk)
        return lax.dot_general(part, rows, NT, preferred_element_type=jnp.float32)

    def own_half():
        for k in range(NX):
            arrived(("os", k), own_piece(k, 1 - c))
        acc[...] = project(0, 0)
        for kc in range(1, KC):
            acc[...] += project(kc, 0)
        spread(h)

    def other_half(kc):
        for k in range(NX):
            arrived(("cs", kc, k), far_piece(kc, k, 1 - c))
        if kc == 0:
            acc[...] = project(kc, 1)
        else:
            acc[...] += project(kc, 1)

    def spread(half):
        for slab in range(NX):
            part = acc[:, slab * 128 : (slab + 1) * 128]
            qb[2 * slab + half] = part[0:128]
            mixed = (part[128:256] * part[256:384]).astype(jnp.bfloat16)
            mx[1 + 2 * slab + half] = mixed.astype(jnp.float32)

    last_w = max(when for when, _ in events if when < 17.0)
    events.append((17.5, own_half))
    for kc in range(KC):
        events.append((max(17.6 + 0.01 * kc, 6.0 + 4.0 * (kc + 1) + 5.0), lambda kc=kc: other_half(kc)))
    events.append((2.1, skips))
    for j in range(16):
        events.append((2.2 + 0.5 * j, lambda j=j: table(j)))
    for _, event in sorted(events, key=lambda e: e[0]):
        event()

    spread(1 - h)
    edge_out[...] = mx[2 * NX].astype(jnp.bfloat16)
    send(("edge",), edge_out, edge_in, after)
    arrived(("edge",), edge_in)
    before_first = edge_in[...].astype(jnp.float32)
    mx[0] = jnp.where(g == 0, jnp.zeros_like(before_first), before_first)

    blocks = 2 * NX
    for j in range(16):
        rows = slice(8 * j, 8 * j + 8)
        now = mx[1 : 1 + blocks, rows, :]
        window = jnp.concatenate([mx[0:blocks, rows, :], now], axis=2)
        window = window.reshape(8 * blocks, 2 * taps).astype(jnp.bfloat16)
        conv = jnp.dot(window, toep[j], preferred_element_type=jnp.float32)
        direct = skip_b[j, pl.ds(x, 1)] * now
        gated = qb[:, rows, :] * (conv.reshape(blocks, 8, taps) + direct)
        gated = gated.reshape(NX, 2, 8, taps).astype(jnp.bfloat16)
        send_out[:, j, :, 0:taps] = gated[:, 0]
        send_out[:, j, :, taps : 2 * taps] = gated[:, 1]

    for k in (2, 1, 3):
        send(("out", k), send_out.at[(x + k) % NX], got.at[:, x], xpeer(k))
    got[:, x] = send_out[x]
    for k in range(1, NX):
        arrived(("out", k), got.at[:, (x + NX - k) % NX])
    out_ref[...] = got[...].astype(jnp.float32).reshape(out_ref.shape).astype(jnp.bfloat16)
    for one in sends:
        one.wait_send()


def shards(tokens, norm_gain, in_weight, filter_taps, skip_gain):
    rows, din = tokens.shape
    taps = filter_taps.shape[1]
    wide = skip_gain.shape[0]
    count = len(CH)
    vmem = pl.BlockSpec(memory_space=pltpu.VMEM)
    out = pl.pallas_call(
        kernel,
        out_shape=jax.ShapeDtypeStruct((wide, 4 * rows), jnp.bfloat16),
        in_specs=[vmem] * 5,
        out_specs=vmem,
        scratch_shapes=[
            pltpu.VMEM((KC, 2, NX, 2, rows, din // KC), jnp.bfloat16),
            pltpu.VMEM((NY * NZ, 8, din), jnp.bfloat16),
            pltpu.VMEM((8 * NY * NZ, NX * 2 * rows), jnp.float32),
            pltpu.VMEM((16, 2 * taps, taps), jnp.bfloat16),
            pltpu.VMEM((16, NX, 8, 128), jnp.float32),
            pltpu.VMEM((2 * NX, 128, 2 * rows), jnp.float32),
            pltpu.VMEM((2 * NX + 1, 128, 2 * rows), jnp.float32),
            pltpu.VMEM((128, 2 * rows), jnp.bfloat16),
            pltpu.VMEM((128, 2 * rows), jnp.bfloat16),
            pltpu.VMEM((NX, 16, 8, 4 * rows), jnp.bfloat16),
            pltpu.VMEM((16, NX, 8, 4 * rows), jnp.bfloat16),
            pltpu.SemaphoreType.DMA((count,)),
            pltpu.SemaphoreType.DMA((count,)),
        ],
        compiler_params=pltpu.CompilerParams(
            collective_id=0, has_side_effects=True, vmem_limit_bytes=40 * 2**20
        ),
    )(tokens, norm_gain.reshape(1, din), in_weight.T, filter_taps, skip_gain.reshape(1, wide))
    return out.T


def solution(mesh):
    return jax.shard_map(
        shards,
        mesh=mesh,
        in_specs=(P(("fsdp", "tp"), None), P(), P(None, ("fsdp", "tp")), P("tp", None), P("tp")),
        out_specs=P("fsdp", "tp"),
        check_vma=False,
    )
```

```python
import functools

import jax
import jax.numpy as jnp
from jax import lax
from jax.experimental import pallas as pl
from jax.experimental.pallas import tpu as pltpu
from jax.sharding import PartitionSpec as P

MESH = pl.DeviceIdType.MESH
NX, NY, NZ = 4, 8, 6
KC = 8
Y_DEPTH = 4
CROSS_DEPTH = 2
GROUP = 2
OWN_AT = 7
OX_AT = 2
NT = (((1,), (1,)), ((), ()))


def reach(direction, d):
    return (4 if d < 3 else 3) if direction > 0 else (3 if d < 3 else 4)


def channels():
    names = [("wz", d) for d in range(NZ)] + [("ws", n) for n in range(NY * NZ)]
    for d in range(NZ):
        for direction in (1, -1):
            names += [("wy", direction, s, d) for s in range(1, reach(direction, d) + 1)]
    names += [("w0",), ("t0",)] + [("ox", k) for k in range(1, NX)] + [("os", k) for k in range(NX)]
    for kc in range(KC):
        names += [("cr", kc)]
        names += [("cx", kc, k) for k in range(1, NX)] + [("cs", kc, k) for k in range(NX)]
    names += [("edge",)] + [("out", k) for k in range(NX)]
    return {name: i for i, name in enumerate(names)}


CH = channels()


def y_order():
    first = [(1, 0), (2, 0), (3, 0), (1, 1), (1, 2), (4, 0), (1, 3), (1, 4), (1, 5)]
    return first + [(s, d) for s in (2, 3, 4) for d in range(1, NZ)]


def kernel(
    tokens_hbm, gain_hbm, w_hbm, taps_hbm, skip_hbm, out_ref,
    tokens_ref, gain_ref, taps_ref, skip_ref,
    tb, wb, acc, toep, skip_b, qb, mx, edge_out, edge_in, send_out, got, ssem, rsem, lsem, ready,
):
    f = lax.axis_index("fsdp")
    t = lax.axis_index("tp")
    x = f % NX
    g = f // NX
    zl = g % NZ
    y = g // NZ
    h = t // 2
    c = t % 2
    taps = taps_ref.shape[1]
    chunk = tb.shape[-1]

    def dev(y_, zl_, x_, h_, c_):
        return ((y_ * NZ + zl_) * NX + x_, h_ * 2 + c_)

    def zpeer(d):
        return dev(y, (zl + d) % NZ, x, h, c)

    def ypeer(d):
        return dev((y + d + NY) % NY, zl, x, h, c)

    def xpeer(k):
        return dev(y, zl, (x + k) % NX, h, c)

    sibling = dev(y, zl, x, h, 1 - c)
    partner = dev(y, zl, x, 1 - h, c)
    g_next = (g + 1) % (NY * NZ)
    g_prev = (g + NY * NZ - 1) % (NY * NZ)
    after = dev(g_next // NZ, g_next % NZ, x, h, c)
    before = dev(g_prev // NZ, g_prev % NZ, x, h, c)

    barrier = pltpu.get_barrier_semaphore()
    shared = [xpeer(k) for k in range(1, NX)] + [sibling]
    for_weight = [zpeer(d) for d in range(1, NZ)] + [ypeer(1), ypeer(-1)]

    def greet(peers):
        for peer in peers:
            pl.semaphore_signal(barrier, inc=1, device_id=peer, device_id_type=MESH)

    greet(shared + [before])

    @pl.when(c == 0)
    def _():
        greet(for_weight)

    @pl.when((c == 1) & (h == 0))
    def _():
        greet([partner])

    loads = [
        pltpu.make_async_copy(tokens_hbm, tokens_ref, lsem.at[0]),
        pltpu.make_async_copy(gain_hbm, gain_ref, lsem.at[1]),
        pltpu.make_async_copy(w_hbm, wb.at[g, c], lsem.at[2]),
        pltpu.make_async_copy(taps_hbm, taps_ref, lsem.at[3]),
        pltpu.make_async_copy(skip_hbm, skip_ref, lsem.at[4]),
    ]
    for load in loads:
        load.start()

    unsent = {}

    def copy(name, src, dst, to, at=None):
        return pltpu.make_async_remote_copy(
            src_ref=src, dst_ref=dst, send_sem=ssem.at[CH[name]],
            recv_sem=rsem.at[CH[name] if at is None else at], device_id=to, device_id_type=MESH,
        )

    def send(name, src, dst, to, at=None):
        one = copy(name, src, dst, to, at)
        one.start()
        unsent[name] = one

    def sent(name):
        if name in unsent:
            unsent.pop(name).wait_send()

    def all_sent():
        for name in list(unsent):
            sent(name)

    def arrived(name, dst, at=None):
        copy(name, dst, dst, sibling, at).wait_recv()

    loads[0].wait()
    loads[1].wait()
    features = tokens_ref[...].astype(jnp.float32)
    power = jnp.mean(features * features, axis=1, keepdims=True)
    normed = (features * lax.rsqrt(power + 1e-06) * gain_ref[...]).astype(jnp.bfloat16)
    for kc in range(KC):
        tb[kc, 0, x, c] = normed[:, kc * chunk : (kc + 1) * chunk]
    loads[2].wait()

    pl.semaphore_wait(barrier, len(shared) + 1 + jnp.where(c == 0, len(for_weight), h))

    row_at = lax.broadcasted_iota(jnp.int32, (taps, taps), 0)
    lane_at = lax.broadcasted_iota(jnp.int32, (taps, taps), 1)

    def tables():
        loads[3].wait()
        loads[4].wait()
        wide = jnp.broadcast_to(skip_ref[...], (128, skip_ref.shape[1]))
        skip_b[...] = wide.T.reshape(skip_b.shape)
        for j in range(16):
            one = taps_ref[pl.ds(2 * j + x // 2, 1), :]
            rolled = pltpu.roll(jnp.broadcast_to(one, (taps, taps)), 0, 1, stride=1, stride_axis=0)
            toep[j, 0:taps] = jnp.where(lane_at < row_at, rolled, 0.0).astype(jnp.bfloat16)
            toep[j, taps : 2 * taps] = jnp.where(lane_at >= row_at, rolled, 0.0).astype(jnp.bfloat16)

    def project(group, which):
        total = None
        for kc in range(group * GROUP, (group + 1) * GROUP):
            rows = tb[kc, which].reshape(-1, chunk)
            part = wb[:, c, :, kc * chunk : (kc + 1) * chunk].reshape(-1, chunk)
            term = lax.dot_general(part, rows, NT, preferred_element_type=jnp.float32)
            total = term if total is None else total + term
        return total

    def spread(half):
        for slab in range(NX):
            part = acc[:, slab * 128 : (slab + 1) * 128]
            qb[2 * slab + half] = part[0:128]
            mixed = (part[128:256] * part[256:384]).astype(jnp.bfloat16)
            mx[1 + 2 * slab + half] = mixed.astype(jnp.float32)

    def edge_copy():
        return copy(("edge",), edge_out, edge_in, after)

    def edge_send():
        edge_out[...] = mx[2 * NX].astype(jnp.bfloat16)
        edge_copy().start()

    def own_half():
        acc[...] = project(0, 0)
        for group in range(1, KC // GROUP):
            acc[...] += project(group, 0)
        spread(h)
        pl.when(h == 1)(edge_send)

    def column(d):
        return zl if d == 0 else jnp.where(d - 1 >= zl, d, d - 1)

    def place(y_, d):
        return (y_ + NY) % NY * NZ + column(d)

    def weight_role():
        def hand_on(n, key):
            send(("ws", key), wb.at[n, 1], wb.at[n, 1], sibling, CH[("ws", 0)] + n)

        keys = iter(range(NY * NZ))
        seen = set()

        def pass_on(direction, s, d):
            n = place(y - direction * (s - 1), d)
            if s > 1:
                arrived(("wy", direction, s - 1, d), wb.at[n])
            elif d and d not in seen:
                arrived(("wz", d), wb.at[n], CH[("wz", 0)] + column(d))
            if s <= reach(direction, d):
                at = order[direction].index((s, d))
                if at >= Y_DEPTH:
                    sent(("wy", direction, *order[direction][at - Y_DEPTH]))
                send(("wy", direction, s, d), wb.at[n], wb.at[n], ypeer(direction))
            if s > 1 or (d and d not in seen):
                hand_on(n, next(keys))
            seen.add(d)

        order = {a: [(s, d) for s, d in y_order() if s <= reach(a, d)] for a in (1, -1)}
        arrived(("w0",), wb.at[g, 1])
        own = wb.at[g]
        for d in range(1, NZ):
            send(("wz", d), own, own, zpeer(d), CH[("wz", 0)] + zl)
        pass_on(1, 1, 0)
        pass_on(-1, 1, 0)
        tables()
        for s, d in y_order()[1:] + [(5, d) for d in range(NZ)]:
            for direction in (1, -1):
                if s <= reach(direction, d) + 1:
                    pass_on(direction, s, d)

    def own_piece(k):
        return tb.at[:, 0, (x + NX - k) % NX]

    def far_piece(kc, k):
        return tb.at[kc, 1, (x + NX - k) % NX]

    def token_role():
        def on_ox(k):
            piece = own_piece(k)
            arrived(("ox", k), piece)
            send(("os", k), piece, piece, sibling)

        def cross(kc):
            if kc >= CROSS_DEPTH:
                sent(("cr", kc - CROSS_DEPTH))
            send(("cr", kc), tb.at[kc, 0, x], tb.at[kc, 1, x], partner)

        def on_cr(kc):
            piece = far_piece(kc, 0)
            arrived(("cr", kc), piece)
            for k in (2, 1, 3):
                send(("cx", kc, k), piece, piece, xpeer(k))
            send(("cs", kc, 0), piece, piece, sibling)

        def on_cx(kc, k):
            piece = far_piece(kc, k)
            arrived(("cx", kc, k), piece)
            send(("cs", kc, k), piece, piece, sibling)

        arrived(("t0",), tb.at[:, 0, x, 0])
        for k in (2, 1, 3):
            send(("ox", k), own_piece(0), own_piece(0), xpeer(k))

        @pl.when(h == 0)
        def _():
            pl.semaphore_wait(ready, 1)

        tables()
        for kc in range(CROSS_DEPTH):
            cross(kc)
        for kc in range(KC):
            on_cr(kc)
            if kc + CROSS_DEPTH < KC:
                cross(kc + CROSS_DEPTH)
            if kc >= 1:
                for k in (1, 3, 2):
                    on_cx(kc - 1, k)
            if kc == OWN_AT:
                for d in range(NY * NZ - 1):
                    n = jnp.where(d >= g, d + 1, d)
                    arrived(("ws", 0), wb.at[n, 1], CH[("ws", 0)] + n)
                own_half()
            if kc == OX_AT:
                for k in (1, 3, 2):
                    on_ox(k)
        for k in (1, 3, 2):
            on_cx(KC - 1, k)

    @pl.when((c == 1) & (h == 1))
    def _():
        pl.semaphore_signal(ready, inc=1, device_id=partner, device_id_type=MESH)

    @pl.when(c == 0)
    def _():
        send(("t0",), tb.at[:, 0, x, 0], tb.at[:, 0, x, 0], sibling)
        weight_role()
        arrived(("os", 0), tb.at[:, 0, x, 1])
        for k in range(1, NX):
            arrived(("os", k), own_piece(k))
        all_sent()
        own_half()

    @pl.when(c == 1)
    def _():
        send(("w0",), wb.at[g, 1], wb.at[g, 1], sibling)
        send(("os", 0), tb.at[:, 0, x, 1], tb.at[:, 0, x, 1], sibling)
        token_role()
        all_sent()

    for group in range(KC // GROUP):
        @pl.when(c == 0)
        def _(group=group):
            for kc in range(group * GROUP, (group + 1) * GROUP):
                for k in range(NX):
                    arrived(("cs", kc, k), far_piece(kc, k))

        if group == 0:
            acc[...] = project(group, 1)
        else:
            acc[...] += project(group, 1)
    spread(1 - h)

    pl.when(h == 0)(edge_send)

    def convolve(j, first, last):
        rows = slice(8 * j, 8 * j + 8)
        now = mx[1 + first : 1 + last, rows, :]
        window = jnp.concatenate([mx[first:last, rows, :], now], axis=2)
        window = window.reshape(8 * (last - first), 2 * taps).astype(jnp.bfloat16)
        conv = jnp.dot(window, toep[j], preferred_element_type=jnp.float32)
        direct = skip_b[j, pl.ds(x, 1)] * now
        gated = qb[first:last, rows, :] * (conv.reshape(last - first, 8, taps) + direct)
        return gated.astype(jnp.bfloat16)

    def out_copy(slab):
        at = CH[("out", 0)] + x
        return copy(("out", slab), send_out.at[slab], got.at[:, x], dev(y, zl, slab, h, c), at)

    def out_send(slab):
        @pl.when(x != slab)
        def _():
            out_copy(slab).start()

    for j in range(16):
        gated = convolve(j, 1, 2 * NX)
        for b in range(1, 2 * NX):
            send_out[b // 2, j, :, b % 2 * taps : (b % 2 + 1) * taps] = gated[b - 1]
    for slab in range(1, NX):
        out_send(slab)
    arrived(("edge",), edge_in)
    before_first = edge_in[...].astype(jnp.float32)
    mx[0] = jnp.where(g == 0, jnp.zeros_like(before_first), before_first)
    for j in range(16):
        send_out[0, j, :, 0:taps] = convolve(j, 0, 1)[0]
    out_send(0)
    got[:, x] = send_out[x]
    for k in range(1, NX):
        source = (x + NX - k) % NX
        arrived(("out", k), got.at[:, source], CH[("out", 0)] + source)
    out_ref[...] = got[...].astype(jnp.float32).reshape(out_ref.shape).astype(jnp.bfloat16)
    for slab in range(NX):
        @pl.when(x != slab)
        def _(slab=slab):
            out_copy(slab).wait_send()

    edge_copy().wait_send()
    all_sent()


def shards(tokens, norm_gain, in_weight, filter_taps, skip_gain):
    rows, din = tokens.shape
    taps = filter_taps.shape[1]
    wide = skip_gain.shape[0]
    count = len(CH)
    hbm = pl.BlockSpec(memory_space=pl.ANY)
    out = pl.pallas_call(
        kernel,
        out_shape=jax.ShapeDtypeStruct((wide, 4 * rows), jnp.bfloat16),
        in_specs=[hbm] * 5,
        out_specs=pl.BlockSpec(memory_space=pltpu.VMEM),
        scratch_shapes=[
            pltpu.VMEM((rows, din), jnp.bfloat16),
            pltpu.VMEM((1, din), jnp.float32),
            pltpu.VMEM(filter_taps.shape, jnp.float32),
            pltpu.VMEM((1, wide), jnp.float32),
            pltpu.VMEM((KC, 2, NX, 2, rows, din // KC), jnp.bfloat16),
            pltpu.VMEM((NY * NZ, 2, 8, din), jnp.bfloat16),
            pltpu.VMEM((8 * NY * NZ, NX * 2 * rows), jnp.float32),
            pltpu.VMEM((16, 2 * taps, taps), jnp.bfloat16),
            pltpu.VMEM((16, NX, 8, 128), jnp.float32),
            pltpu.VMEM((2 * NX, 128, 2 * rows), jnp.float32),
            pltpu.VMEM((2 * NX + 1, 128, 2 * rows), jnp.float32),
            pltpu.VMEM((128, 2 * rows), jnp.bfloat16),
            pltpu.VMEM((128, 2 * rows), jnp.bfloat16),
            pltpu.VMEM((NX, 16, 8, 4 * rows), jnp.bfloat16),
            pltpu.VMEM((16, NX, 8, 4 * rows), jnp.bfloat16),
            pltpu.SemaphoreType.DMA((count,)),
            pltpu.SemaphoreType.DMA((count,)),
            pltpu.SemaphoreType.DMA((5,)),
            pltpu.SemaphoreType.REGULAR,
        ],
        compiler_params=pltpu.CompilerParams(
            collective_id=0, has_side_effects=True, vmem_limit_bytes=56 * 2**20
        ),
    )(tokens, norm_gain.reshape(1, din), in_weight.T, filter_taps, skip_gain.reshape(1, wide))
    return out.T


def solution(mesh):
    return jax.shard_map(
        shards,
        mesh=mesh,
        in_specs=(P(("fsdp", "tp"), None), P(), P(None, ("fsdp", "tp")), P("tp", None), P("tp")),
        out_specs=P("fsdp", "tp"),
        check_vma=False,
    )
```

```python
import functools

import jax
import jax.numpy as jnp
from jax import lax
from jax.experimental import pallas as pl
from jax.experimental.pallas import tpu as pltpu
from jax.sharding import PartitionSpec as P

MESH = pl.DeviceIdType.MESH
NX, NY, NZ = 4, 8, 6
KC = 8
Y_DEPTH = 4
EARLY_DEPTH = 1
LATE_DEPTH = 4
GROUP = 2
OWN_AT = 7
OX_AT = 2
NT = (((1,), (1,)), ((), ()))


def reach(direction, d):
    return (4 if d < 3 else 3) if direction > 0 else (3 if d < 3 else 4)


def channels():
    names = [("wz", d) for d in range(NZ)] + [("ws", n) for n in range(NY * NZ)]
    for d in range(NZ):
        for direction in (1, -1):
            names += [("wy", direction, s, d) for s in range(1, reach(direction, d) + 1)]
    names += [("w0",), ("t0",)] + [("ox", k) for k in range(1, NX)] + [("os", k) for k in range(NX)]
    for kc in range(KC):
        names += [("cr", kc)]
        names += [("cx", kc, k) for k in range(1, NX)] + [("cs", kc, k) for k in range(NX)]
    names += [("edge",)] + [("out", k) for k in range(NX)]
    return {name: i for i, name in enumerate(names)}


CH = channels()


def y_order():
    first = [(1, 0), (2, 0), (3, 0), (1, 1), (1, 2), (4, 0), (1, 3), (1, 4), (1, 5)]
    return first + [(s, d) for s in (2, 3, 4) for d in range(1, NZ)]


def kernel(
    tokens_hbm, gain_hbm, w_hbm, taps_hbm, skip_hbm, out_ref,
    tokens_ref, gain_ref, taps_ref, skip_ref,
    tb, wb, acc, toep, skip_b, qb, mx, edge_out, edge_in, send_out, ssem, rsem, lsem, ready,
):
    f = lax.axis_index("fsdp")
    t = lax.axis_index("tp")
    x = f % NX
    g = f // NX
    zl = g % NZ
    y = g // NZ
    h = t // 2
    c = t % 2
    taps = taps_ref.shape[1]
    chunk = tb.shape[-1]

    def dev(y_, zl_, x_, h_, c_):
        return ((y_ * NZ + zl_) * NX + x_, h_ * 2 + c_)

    def zpeer(d):
        return dev(y, (zl + d) % NZ, x, h, c)

    def ypeer(d):
        return dev((y + d + NY) % NY, zl, x, h, c)

    def xpeer(k):
        return dev(y, zl, (x + k) % NX, h, c)

    sibling = dev(y, zl, x, h, 1 - c)
    partner = dev(y, zl, x, 1 - h, c)
    g_next = (g + 1) % (NY * NZ)
    g_prev = (g + NY * NZ - 1) % (NY * NZ)
    after = dev(g_next // NZ, g_next % NZ, x, h, c)
    before = dev(g_prev // NZ, g_prev % NZ, x, h, c)

    barrier = pltpu.get_barrier_semaphore()
    shared = [xpeer(k) for k in range(1, NX)] + [sibling]
    for_weight = [zpeer(d) for d in range(1, NZ)] + [ypeer(1), ypeer(-1)]

    def greet(peers):
        for peer in peers:
            pl.semaphore_signal(barrier, inc=1, device_id=peer, device_id_type=MESH)

    greet(shared + [before])

    @pl.when(c == 0)
    def _():
        greet(for_weight)

    @pl.when((c == 1) & (h == 0))
    def _():
        greet([partner])

    loads = [
        pltpu.make_async_copy(tokens_hbm, tokens_ref, lsem.at[0]),
        pltpu.make_async_copy(gain_hbm, gain_ref, lsem.at[1]),
        pltpu.make_async_copy(w_hbm, wb.at[g, c], lsem.at[2]),
        pltpu.make_async_copy(taps_hbm, taps_ref, lsem.at[3]),
        pltpu.make_async_copy(skip_hbm, skip_ref, lsem.at[4]),
    ]
    for load in loads:
        load.start()

    unsent = {}

    def copy(name, src, dst, to, at=None):
        return pltpu.make_async_remote_copy(
            src_ref=src, dst_ref=dst, send_sem=ssem.at[CH[name]],
            recv_sem=rsem.at[CH[name] if at is None else at], device_id=to, device_id_type=MESH,
        )

    def send(name, src, dst, to, at=None):
        one = copy(name, src, dst, to, at)
        one.start()
        unsent[name] = one

    def sent(name):
        if name in unsent:
            unsent.pop(name).wait_send()

    def all_sent():
        for name in list(unsent):
            sent(name)

    def arrived(name, dst, at=None):
        copy(name, dst, dst, sibling, at).wait_recv()

    loads[0].wait()
    loads[1].wait()
    features = tokens_ref[...].astype(jnp.float32)
    power = jnp.mean(features * features, axis=1, keepdims=True)
    normed = (features * lax.rsqrt(power + 1e-06) * gain_ref[...]).astype(jnp.bfloat16)
    for kc in range(KC):
        tb[kc, 0, x, c] = normed[:, kc * chunk : (kc + 1) * chunk]
    loads[2].wait()

    pl.semaphore_wait(barrier, len(shared) + 1 + jnp.where(c == 0, len(for_weight), h))

    row_at = lax.broadcasted_iota(jnp.int32, (taps, taps), 0)
    lane_at = lax.broadcasted_iota(jnp.int32, (taps, taps), 1)

    def tables():
        loads[3].wait()
        loads[4].wait()
        wide = jnp.broadcast_to(skip_ref[...], (128, skip_ref.shape[1]))
        skip_b[...] = wide.T.reshape(skip_b.shape)
        for j in range(16):
            one = taps_ref[pl.ds(2 * j + x // 2, 1), :]
            rolled = pltpu.roll(jnp.broadcast_to(one, (taps, taps)), 0, 1, stride=1, stride_axis=0)
            toep[j, 0:taps] = jnp.where(lane_at < row_at, rolled, 0.0).astype(jnp.bfloat16)
            toep[j, taps : 2 * taps] = jnp.where(lane_at >= row_at, rolled, 0.0).astype(jnp.bfloat16)

    def project(group, which):
        total = None
        for kc in range(group * GROUP, (group + 1) * GROUP):
            rows = tb[kc, which].reshape(-1, chunk)
            part = wb[:, c, :, kc * chunk : (kc + 1) * chunk].reshape(-1, chunk)
            term = lax.dot_general(part, rows, NT, preferred_element_type=jnp.float32)
            total = term if total is None else total + term
        return total

    def spread(half):
        for slab in range(NX):
            part = acc[:, slab * 128 : (slab + 1) * 128]
            qb[2 * slab + half] = part[0:128]
            mixed = (part[128:256] * part[256:384]).astype(jnp.bfloat16)
            mx[1 + 2 * slab + half] = mixed.astype(jnp.float32)

    def edge_copy():
        return copy(("edge",), edge_out, edge_in, after)

    def edge_send():
        edge_out[...] = mx[2 * NX].astype(jnp.bfloat16)
        edge_copy().start()

    def own_half():
        acc[...] = project(0, 0)
        for group in range(1, KC // GROUP):
            acc[...] += project(group, 0)
        spread(h)
        pl.when(h == 1)(edge_send)

    def column(d):
        return zl if d == 0 else jnp.where(d - 1 >= zl, d, d - 1)

    def place(y_, d):
        return (y_ + NY) % NY * NZ + column(d)

    def weight_role():
        def hand_on(n, key):
            send(("ws", key), wb.at[n, 1], wb.at[n, 1], sibling, CH[("ws", 0)] + n)

        keys = iter(range(NY * NZ))
        seen = set()

        def pass_on(direction, s, d):
            n = place(y - direction * (s - 1), d)
            if s > 1:
                arrived(("wy", direction, s - 1, d), wb.at[n])
            elif d and d not in seen:
                arrived(("wz", d), wb.at[n], CH[("wz", 0)] + column(d))
            if s <= reach(direction, d):
                at = order[direction].index((s, d))
                if at >= Y_DEPTH:
                    sent(("wy", direction, *order[direction][at - Y_DEPTH]))
                send(("wy", direction, s, d), wb.at[n], wb.at[n], ypeer(direction))
            if s > 1 or (d and d not in seen):
                hand_on(n, next(keys))
            seen.add(d)

        order = {a: [(s, d) for s, d in y_order() if s <= reach(a, d)] for a in (1, -1)}
        arrived(("w0",), wb.at[g, 1])
        own = wb.at[g]
        for d in range(1, NZ):
            send(("wz", d), own, own, zpeer(d), CH[("wz", 0)] + zl)
        pass_on(1, 1, 0)
        pass_on(-1, 1, 0)
        tables()
        for s, d in y_order()[1:] + [(5, d) for d in range(NZ)]:
            for direction in (1, -1):
                if s <= reach(direction, d) + 1:
                    pass_on(direction, s, d)

    def own_piece(k):
        return tb.at[:, 0, (x + NX - k) % NX]

    def far_piece(kc, k):
        return tb.at[kc, 1, (x + NX - k) % NX]

    def token_role():
        def on_ox(k):
            piece = own_piece(k)
            arrived(("ox", k), piece)
            send(("os", k), piece, piece, sibling)

        def cross_copy(kc):
            return copy(("cr", kc), tb.at[kc, 0, x], tb.at[kc, 1, x], partner)

        depths = ((0, EARLY_DEPTH), (1, LATE_DEPTH))

        def cross_next(kc):
            for half, depth in depths:
                @pl.when(h == half)
                def _(depth=depth):
                    cross_copy(kc).wait_send()
                    if kc + depth < KC:
                        cross_copy(kc + depth).start()

        def on_cr(kc):
            piece = far_piece(kc, 0)
            arrived(("cr", kc), piece)
            for k in (2, 1, 3):
                send(("cx", kc, k), piece, piece, xpeer(k))
            send(("cs", kc, 0), piece, piece, sibling)

        def on_cx(kc, k):
            piece = far_piece(kc, k)
            arrived(("cx", kc, k), piece)
            send(("cs", kc, k), piece, piece, sibling)

        arrived(("t0",), tb.at[:, 0, x, 0])
        for k in (2, 1, 3):
            send(("ox", k), own_piece(0), own_piece(0), xpeer(k))

        @pl.when(h == 0)
        def _():
            pl.semaphore_wait(ready, 1)

        tables()
        for half, depth in depths:
            @pl.when(h == half)
            def _(depth=depth):
                for kc in range(depth):
                    cross_copy(kc).start()

        for kc in range(KC):
            on_cr(kc)
            cross_next(kc)
            if kc >= 1:
                for k in (1, 3, 2):
                    on_cx(kc - 1, k)
            if kc == OWN_AT:
                for d in range(NY * NZ - 1):
                    n = jnp.where(d >= g, d + 1, d)
                    arrived(("ws", 0), wb.at[n, 1], CH[("ws", 0)] + n)
                own_half()
            if kc == OX_AT:
                for k in (1, 3, 2):
                    on_ox(k)
        for k in (1, 3, 2):
            on_cx(KC - 1, k)

    @pl.when((c == 1) & (h == 1))
    def _():
        pl.semaphore_signal(ready, inc=1, device_id=partner, device_id_type=MESH)

    @pl.when(c == 0)
    def _():
        send(("t0",), tb.at[:, 0, x, 0], tb.at[:, 0, x, 0], sibling)
        weight_role()
        arrived(("os", 0), tb.at[:, 0, x, 1])
        for k in range(1, NX):
            arrived(("os", k), own_piece(k))
        all_sent()
        own_half()

    @pl.when(c == 1)
    def _():
        send(("w0",), wb.at[g, 1], wb.at[g, 1], sibling)
        send(("os", 0), tb.at[:, 0, x, 1], tb.at[:, 0, x, 1], sibling)
        token_role()
        all_sent()

    for group in range(KC // GROUP):
        @pl.when(c == 0)
        def _(group=group):
            for kc in range(group * GROUP, (group + 1) * GROUP):
                for k in range(NX):
                    arrived(("cs", kc, k), far_piece(kc, k))

        if group == 0:
            acc[...] = project(group, 1)
        else:
            acc[...] += project(group, 1)
    spread(1 - h)

    pl.when(h == 0)(edge_send)

    def convolve(j, first, last):
        rows = slice(8 * j, 8 * j + 8)
        now = mx[1 + first : 1 + last, rows, :]
        window = jnp.concatenate([mx[first:last, rows, :], now], axis=2)
        window = window.reshape(8 * (last - first), 2 * taps).astype(jnp.bfloat16)
        conv = jnp.dot(window, toep[j], preferred_element_type=jnp.float32)
        direct = skip_b[j, pl.ds(x, 1)] * now
        gated = qb[first:last, rows, :] * (conv.reshape(last - first, 8, taps) + direct)
        return gated.astype(jnp.bfloat16)

    def out_copy(slab):
        at = CH[("out", 0)] + x
        return copy(("out", slab), send_out.at[slab], out_ref.at[:, x], dev(y, zl, slab, h, c), at)

    def out_send(slab):
        @pl.when(x != slab)
        def _():
            out_copy(slab).start()

    for j in range(16):
        gated = convolve(j, 1, 2 * NX)
        for b in range(1, 2 * NX):
            send_out[b // 2, j, :, b % 2 * taps : (b % 2 + 1) * taps] = gated[b - 1]
    for slab in range(1, NX):
        out_send(slab)
    arrived(("edge",), edge_in)
    before_first = edge_in[...].astype(jnp.float32)
    mx[0] = jnp.where(g == 0, jnp.zeros_like(before_first), before_first)
    for j in range(16):
        send_out[0, j, :, 0:taps] = convolve(j, 0, 1)[0]
    out_send(0)
    own_out = pltpu.make_async_copy(send_out.at[x], out_ref.at[:, x], lsem.at[0])
    own_out.start()
    for k in range(1, NX):
        source = (x + NX - k) % NX
        arrived(("out", k), out_ref.at[:, source], CH[("out", 0)] + source)
    own_out.wait()
    for slab in range(NX):
        @pl.when(x != slab)
        def _(slab=slab):
            out_copy(slab).wait_send()

    edge_copy().wait_send()
    all_sent()


def shards(tokens, norm_gain, in_weight, filter_taps, skip_gain):
    rows, din = tokens.shape
    taps = filter_taps.shape[1]
    wide = skip_gain.shape[0]
    count = len(CH)
    hbm = pl.BlockSpec(memory_space=pl.ANY)
    out = pl.pallas_call(
        kernel,
        out_shape=jax.ShapeDtypeStruct((16, NX, 8, 4 * rows), jnp.bfloat16),
        in_specs=[hbm] * 5,
        out_specs=hbm,
        scratch_shapes=[
            pltpu.VMEM((rows, din), jnp.bfloat16),
            pltpu.VMEM((1, din), jnp.float32),
            pltpu.VMEM(filter_taps.shape, jnp.float32),
            pltpu.VMEM((1, wide), jnp.float32),
            pltpu.VMEM((KC, 2, NX, 2, rows, din // KC), jnp.bfloat16),
            pltpu.VMEM((NY * NZ, 2, 8, din), jnp.bfloat16),
            pltpu.VMEM((8 * NY * NZ, NX * 2 * rows), jnp.float32),
            pltpu.VMEM((16, 2 * taps, taps), jnp.bfloat16),
            pltpu.VMEM((16, NX, 8, 128), jnp.float32),
            pltpu.VMEM((2 * NX, 128, 2 * rows), jnp.float32),
            pltpu.VMEM((2 * NX + 1, 128, 2 * rows), jnp.float32),
            pltpu.VMEM((128, 2 * rows), jnp.bfloat16),
            pltpu.VMEM((128, 2 * rows), jnp.bfloat16),
            pltpu.VMEM((NX, 16, 8, 4 * rows), jnp.bfloat16),
            pltpu.SemaphoreType.DMA((count,)),
            pltpu.SemaphoreType.DMA((count,)),
            pltpu.SemaphoreType.DMA((5,)),
            pltpu.SemaphoreType.REGULAR,
        ],
        compiler_params=pltpu.CompilerParams(
            collective_id=0, has_side_effects=True, vmem_limit_bytes=56 * 2**20
        ),
    )(tokens, norm_gain.reshape(1, din), in_weight.T, filter_taps, skip_gain.reshape(1, wide))
    return out.reshape(wide, 4 * rows).T


def solution(mesh):
    return jax.shard_map(
        shards,
        mesh=mesh,
        in_specs=(P(("fsdp", "tp"), None), P(), P(None, ("fsdp", "tp")), P("tp", None), P("tp")),
        out_specs=P("fsdp", "tp"),
        check_vma=False,
    )
```
